256 devices in a mesh: train: 8 (over z_hi, y), tp: 16 (over z_lo, x), dp: 2 (over core).
Axes of the slice: x: 4, y: 4, z: 8 (z_hi: 2, z_lo: 4; z = z_hi * 4 + z_lo), core: 2. Of those that a mesh axis runs over, the one named last changes fastest.
Arguments:
- adapter_down_factor: bfloat16 [2, 2, 64, 8192], P(None, None, None, ('train', 'tp')), may hold values from -6 to 6
- adapter_up_factor: bfloat16 [2, 2, 1024, 64], P(None, None, ('train', 'tp')), may hold values from -0.75 to 0.75
- projection_weight: bfloat16 [2, 2, 1024, 8192], P(None, None, 'tp'), may hold values from -6 to 6
Outputs:
- merged: bfloat16 [2, 2, 1024, 8192], P(None, None, 'tp')
The draws below stay inside these ranges and needn't reach their ends.
All inputs are finite; a program needn't handle non-finite values.
Results may differ from the reference program's by a relative error of at most 0.001.
Values may be sent and summed in bfloat16 or wider, within the bound.
No kernel may reach another device: no remote copies, remote signals or barrier semaphores. Data moves between devices by JAX's collectives and lax.ppermute only.
A program may use at most 64 MiB of HBM per device.

```python
import jax
import jax.numpy as jnp

MODEL_WIDTH = 8192
KEY_ROWS = 1024
ADAPTER_RANK = 64
DECODER_LAYERS = 2


def level_of(rng, dims, cuts, low, top_value):
    def one(position, parts):
        steps = jax.random.uniform(jax.random.fold_in(jax.random.fold_in(rng, 6), position), (parts,), jnp.float32, low / len(cuts), top_value / len(cuts))
        return jnp.repeat(jnp.exp(steps), dims[position] // parts).reshape((-1,) + (1,) * (len(dims) - position - 1))

    factor_of = one(*cuts[0])
    for cut in cuts[1:]:
        factor_of = factor_of * one(*cut)
    return factor_of


def centred(own_key, dims, scale, most, cuts=(), dtype=jnp.bfloat16):
    entries = jax.random.normal(own_key, dims, jnp.float32) * scale
    if len(cuts) > 0:
        entries = level_of(own_key, dims, cuts, -0.22, 0.18) * entries
    return jnp.clip(entries, min=-most, max=most).astype(dtype)


def setup_inputs(seed: int = 0) -> dict:
    seeds = jax.random.split(jax.random.key(seed), 4)
    adapter_down_factor = centred(seeds[0], (DECODER_LAYERS, 2, ADAPTER_RANK, MODEL_WIDTH), 1.0, 6.0, ((3, 128),))
    adapter_up_factor = centred(seeds[1], (DECODER_LAYERS, 2, KEY_ROWS, ADAPTER_RANK), 0.125, 0.75, ((2, 128),))
    projection_weight = centred(seeds[2], (DECODER_LAYERS, 2, KEY_ROWS, MODEL_WIDTH), 1.0, 6.0, ((2, 16),))
    return dict(adapter_down_factor=adapter_down_factor, adapter_up_factor=adapter_up_factor, projection_weight=projection_weight)


adapter_scale = 2.0


def reference(adapter_down_factor, adapter_up_factor, projection_weight):
    weight_update = jnp.einsum("eitd,eidh->eith", adapter_up_factor.astype(jnp.float32), adapter_down_factor.astype(jnp.float32))
    return (projection_weight.astype(jnp.float32) + adapter_scale * weight_update).astype(jnp.bfloat16)
```

```python
import functools

import jax
import jax.numpy as jnp
from jax import lax
from jax.experimental import pallas as pl
from jax.experimental.pallas import tpu as pltpu
from jax.sharding import PartitionSpec as P


AXES = ("train", "tp", "dp")
NX, NY, NZ = 4, 4, 8
H = 64
UP = 8
ROWS = H + UP
CHUNK = 2048


def linear(x, y, z, c):
    return (((z >> 2) * NY + y) * 16 + (z & 3) * NX + x) * 2 + c


def coords():
    for x in range(NX):
        for y in range(NY):
            for z in range(NZ):
                for c in range(2):
                    yield x, y, z, c


def place(dx, dy, dz):
    return (
        ((dz >> 2) & 1) * 16
        + ((dz >> 1) & 1) * 8
        + ((dx >> 1) & 1) * 4
        + ((dy >> 1) & 1) * 2
        + (dz & 1)
    )


def colour_groups():
    groups = {}
    for x, y, z, c in coords():
        key = ((x ^ z) & 1, (y ^ z) & 1, c)
        groups.setdefault(key, [0] * 32)[place(x, y, z)] = linear(x, y, z, c)
    return list(groups.values())


def from_neighbour(axis):
    pairs = []
    for x, y, z, c in coords():
        q = [x, y, z]
        q[axis] += 1 if c == 0 else -1
        pairs.append((linear(x, y, z, c), linear(q[0] % NX, q[1] % NY, q[2] % NZ, c)))
    return pairs


def other_core():
    return [(linear(x, y, z, c), linear(x, y, z, 1 - c)) for x, y, z, c in coords()]


def merge_kernel(s_ref, a0, a1, a2, a3, w_ref, *rest):
    o_ref, u_ref = rest[-2:]
    lists = (a0, a1, a2, a3)
    mx, my, mz = s_ref[1], s_ref[2], s_ref[3]
    px = (mx ^ mz) & 1
    py = (my ^ mz) & 1

    @pl.when(pl.program_id(0) == 0)
    def _():
        b = (mz & 3) * NX + mx
        y = (b >> 1) & 3
        rows = []
        for j in range(8):
            x = j & 3
            z = (b >> 3) * 4 + (b & 1) * 2 + (j >> 2)
            rel = ((x ^ z ^ px) & 1) + 2 * ((y ^ z ^ py) & 1)
            k = place(x, y, z)
            row = lists[0][k][H:ROWS]
            for i in range(1, 4):
                row = jnp.where(rel == i, lists[i][k][H:ROWS], row)
            rows.append(row.astype(jnp.float32) * 2.0)
        u = jnp.concatenate(rows, axis=0)
        u = jnp.concatenate([u, u], axis=0)
        r = lax.broadcasted_iota(jnp.int32, u.shape, 0) // 64
        c = lax.broadcasted_iota(jnp.int32, u.shape, 1) // 64
        u_ref[...] = jnp.where(r == c, u, 0.0).astype(jnp.bfloat16)

    u = u_ref[...]
    zh = pl.program_id(0) >> 1
    y1 = pl.program_id(0) & 1
    for y0 in range(2):
        y = y1 * 2 + y0
        for z1 in range(2):
            for kind in range(2):
                z0 = py ^ (y0 ^ kind)
                z = zh * 4 + z1 * 2 + z0
                first = px ^ z0
                for xh in range(2):
                    ka = place(2 * xh + first, y, z)
                    kb = place(2 * xh + 1 - first, y, z)
                    a = lists[2 * kind][ka][:H]
                    b = lists[2 * kind + 1][kb][:H]
                    d = jnp.concatenate(
                        [jnp.where(first == 0, a, b), jnp.where(first == 0, b, a)], axis=0
                    )
                    delta = lax.dot_general(
                        u, d, (((1,), (1,)), ((), ())), preferred_element_type=jnp.float32
                    )
                    col = pl.multiple_of((y0 * 8 + z1 * 4 + z0 * 2 + xh) * 128, 128)
                    for p in range(2):
                        w = w_ref[0, p, :, pl.ds(col, 128)].astype(jnp.float32)
                        o_ref[0, p, :, pl.ds(col, 128)] = (
                            w + delta[p * 64 : p * 64 + 64]
                        ).astype(jnp.bfloat16)


def merge(scalars, lists, weight, out=None):
    block = pl.BlockSpec((1, 2, 64, CHUNK), lambda i, s: (s[0], 0, 0, i))
    whole = pl.BlockSpec((32, ROWS, 128), lambda i, s: (0, 0, 0), pipeline_mode=pl.Buffered(1))
    in_specs = [whole] * 4 + [block]
    args = [scalars, *lists, weight]
    aliases = {}
    if out is not None:
        in_specs.append(pl.BlockSpec(memory_space=pl.ANY))
        args.append(out)
        aliases = {6: 0}
    return pl.pallas_call(
        merge_kernel,
        grid_spec=pltpu.PrefetchScalarGridSpec(
            num_scalar_prefetch=1,
            grid=(weight.shape[-1] // CHUNK,),
            in_specs=in_specs,
            out_specs=block,
            scratch_shapes=[pltpu.VMEM((128, 128), jnp.bfloat16)],
        ),
        out_shape=jax.ShapeDtypeStruct(weight.shape, weight.dtype),
        input_output_aliases=aliases,
        compiler_params=pltpu.CompilerParams(vmem_limit_bytes=32 * 1024 * 1024),
        cost_estimate=pl.CostEstimate(
            flops=2 * 128 * 128 * 8192, bytes_accessed=6 * 1024 * 1024, transcendentals=0
        ),
    )(*args)


def solution(mesh):
    groups = colour_groups()

    def local(down, up, weight):
        core = lax.axis_index("dp")
        train = lax.axis_index("train")
        tp = lax.axis_index("tp")
        x = tp % NX
        y = train % NY
        z = (train // NY) * 4 + tp // NX

        d = lax.dynamic_index_in_dim(down, core, 0, keepdims=False).reshape(128, H).T
        u = lax.dynamic_index_in_dim(up, core, 0, keepdims=False)
        u = u.transpose(1, 0, 2).reshape(UP, 128)
        mine = jnp.concatenate([d, u], axis=0)

        many = jnp.broadcast_to(mine[None], (32, ROWS, 128))
        own = lax.all_to_all(many, AXES, 0, 0, axis_index_groups=groups, tiled=True)
        lists = [own] + [lax.ppermute(own, AXES, from_neighbour(a)) for a in range(3)]
        swapped = [lax.ppermute(a, AXES, other_core()) for a in lists]

        here = jnp.stack([core, x, y, z]).astype(jnp.int32)
        there = jnp.stack([1 - core, x, y, z]).astype(jnp.int32)
        out = merge(here, lists, weight)
        return merge(there, swapped, weight, out)

    spec = P(None, None, "tp", None)
    return jax.shard_map(
        local,
        mesh=mesh,
        in_specs=(
            P(None, None, None, ("train", "tp")),
            P(None, None, ("train", "tp"), None),
            spec,
        ),
        out_specs=spec,
        check_vma=False,
    )
```

```python
import jax
import jax.numpy as jnp
from jax import lax
from jax.experimental import pallas as pl
from jax.experimental.pallas import tpu as pltpu
from jax.sharding import PartitionSpec as P


AXES = ("train", "tp", "dp")
NX, NY, NZ = 4, 4, 8
H = 64
UP = 8
ROWS = H + UP
CHUNK = 2048
CHUNKS = 4
VMEM_LIMIT = 16 * 1024 * 1024


def linear(x, y, z, c):
    return (((z >> 2) * NY + y) * 16 + (z & 3) * NX + x) * 2 + c


def coords():
    for x in range(NX):
        for y in range(NY):
            for z in range(NZ):
                for c in range(2):
                    yield x, y, z, c


def place(dx, dy, dz):
    return (
        ((dz >> 2) & 1) * 16
        + ((dz >> 1) & 1) * 8
        + ((dx >> 1) & 1) * 4
        + ((dy >> 1) & 1) * 2
        + (dz & 1)
    )


def colour_groups():
    groups = {}
    for x, y, z, c in coords():
        key = ((x ^ z) & 1, (y ^ z) & 1, c)
        groups.setdefault(key, [0] * 32)[place(x, y, z)] = linear(x, y, z, c)
    return list(groups.values())


def from_neighbour(axis):
    pairs = []
    for x, y, z, c in coords():
        q = [x, y, z]
        q[axis] += 1 if c == 0 else -1
        pairs.append((linear(x, y, z, c), linear(q[0] % NX, q[1] % NY, q[2] % NZ, c)))
    return pairs


def other_core():
    return [(linear(x, y, z, c), linear(x, y, z, 1 - c)) for x, y, z, c in coords()]


def merge_kernel(s_ref, a0, a1, a2, a3, w_ref, *rest):
    o_ref, buf, u_ref, load_sem, store_sem = rest[-5:]
    lists = (a0, a1, a2, a3)
    layer, mx, my, mz = s_ref[0], s_ref[1], s_ref[2], s_ref[3]
    px = (mx ^ mz) & 1
    py = (my ^ mz) & 1

    def part(ref, i):
        return ref.at[layer, :, :, pl.ds(i * CHUNK, CHUNK)]

    def load(i):
        return pltpu.make_async_copy(part(w_ref, i), buf.at[i], load_sem.at[i])

    def store(i):
        return pltpu.make_async_copy(buf.at[i], part(o_ref, i), store_sem.at[i])

    for i in range(CHUNKS):
        load(i).start()

    b = (mz & 3) * NX + mx
    y = (b >> 1) & 3
    rows = []
    for j in range(8):
        x = j & 3
        z = (b >> 3) * 4 + (b & 1) * 2 + (j >> 2)
        rel = ((x ^ z ^ px) & 1) + 2 * ((y ^ z ^ py) & 1)
        k = place(x, y, z)
        row = lists[0][k, H:ROWS]
        for i in range(1, 4):
            row = jnp.where(rel == i, lists[i][k, H:ROWS], row)
        rows.append(row.astype(jnp.float32) * 2.0)
    u = jnp.concatenate(rows, axis=0)
    u = jnp.concatenate([u, u], axis=0)
    r = lax.broadcasted_iota(jnp.int32, u.shape, 0) // 64
    c = lax.broadcasted_iota(jnp.int32, u.shape, 1) // 64
    u_ref[...] = jnp.where(r == c, u, 0.0).astype(jnp.bfloat16)

    for i in range(CHUNKS):
        u = u_ref[...]
        zh, y1 = i >> 1, i & 1
        load(i).wait()
        for y0 in range(2):
            y = y1 * 2 + y0
            for z1 in range(2):
                for kind in range(2):
                    z0 = py ^ (y0 ^ kind)
                    z = zh * 4 + z1 * 2 + z0
                    first = px ^ z0
                    parts = []
                    for xh in range(2):
                        k = place(2 * xh, y, z)
                        even = lists[2 * kind][k, :H]
                        odd = lists[2 * kind + 1][k, :H]
                        parts.append(jnp.where(first == 0, even, odd))
                        parts.append(jnp.where(first == 0, odd, even))
                    delta = lax.dot_general(
                        u,
                        jnp.concatenate(parts, axis=0),
                        (((1,), (1,)), ((), ())),
                        preferred_element_type=jnp.float32,
                    )
                    at = pl.multiple_of((y0 * 4 + z1 * 2 + z0) * 256, 256)
                    for p in range(2):
                        w = buf[i, p, :, pl.ds(at, 256)].astype(jnp.float32)
                        buf[i, p, :, pl.ds(at, 256)] = (
                            w + delta[p * 64 : p * 64 + 64]
                        ).astype(jnp.bfloat16)
        store(i).start()
    for i in range(CHUNKS):
        store(i).wait()


def merge(scalars, lists, weight, out=None):
    inside = pl.BlockSpec(memory_space=pltpu.VMEM)
    outside = pl.BlockSpec(memory_space=pl.ANY)
    in_specs = [pl.BlockSpec(memory_space=pltpu.SMEM)] + [inside] * 4 + [outside]
    args = [scalars, *lists, pltpu.with_memory_space_constraint(weight, pltpu.HBM)]
    aliases = {}
    if out is not None:
        in_specs.append(outside)
        args.append(out)
        aliases = {6: 0}
    return pl.pallas_call(
        merge_kernel,
        in_specs=in_specs,
        out_specs=outside,
        out_shape=jax.ShapeDtypeStruct(weight.shape, weight.dtype),
        scratch_shapes=[
            pltpu.VMEM((CHUNKS, 2, 64, CHUNK), jnp.bfloat16),
            pltpu.VMEM((128, 128), jnp.bfloat16),
            pltpu.SemaphoreType.DMA((CHUNKS,)),
            pltpu.SemaphoreType.DMA((CHUNKS,)),
        ],
        input_output_aliases=aliases,
        compiler_params=pltpu.CompilerParams(vmem_limit_bytes=VMEM_LIMIT),
        cost_estimate=pl.CostEstimate(
            flops=2 * 128 * 128 * 8192, bytes_accessed=6 * 1024 * 1024, transcendentals=0
        ),
    )(*args)


def solution(mesh):
    groups = colour_groups()

    def local(down, up, weight):
        core = lax.axis_index("dp")
        train = lax.axis_index("train")
        tp = lax.axis_index("tp")
        x = tp % NX
        y = train % NY
        z = (train // NY) * 4 + tp // NX

        d = lax.dynamic_index_in_dim(down, core, 0, keepdims=False).reshape(128, H).T
        u = lax.dynamic_index_in_dim(up, core, 0, keepdims=False)
        u = u.transpose(1, 0, 2).reshape(UP, 128)
        mine = jnp.concatenate([d, u], axis=0)

        many = jnp.broadcast_to(mine[None], (32, ROWS, 128))
        own = lax.all_to_all(many, AXES, 0, 0, axis_index_groups=groups, tiled=True)
        lists = [own] + [lax.ppermute(own, AXES, from_neighbour(a)) for a in range(3)]
        swapped = [lax.ppermute(a, AXES, other_core()) for a in lists]

        here = jnp.stack([core, x, y, z]).astype(jnp.int32)
        there = jnp.stack([1 - core, x, y, z]).astype(jnp.int32)
        out = merge(here, lists, weight)
        return merge(there, swapped, weight, out)

    spec = P(None, None, "tp", None)
    return jax.shard_map(
        local,
        mesh=mesh,
        in_specs=(
            P(None, None, None, ("train", "tp")),
            P(None, None, ("train", "tp"), None),
            spec,
        ),
        out_specs=spec,
        check_vma=False,
    )
```

```python
import jax
import jax.numpy as jnp
from jax import lax
from jax.experimental import pallas as pl
from jax.experimental.pallas import tpu as pltpu
from jax.sharding import PartitionSpec as P


AXES = ("train", "tp", "dp")
NX, NY, NZ = 4, 4, 8
H = 64
UP = 8
ROWS = H + UP
CHUNK = 2048
CHUNKS = 4
VMEM_LIMIT = 16 * 1024 * 1024


def linear(x, y, z, c):
    return (((z >> 2) * NY + y) * 16 + (z & 3) * NX + x) * 2 + c


def coords():
    for x in range(NX):
        for y in range(NY):
            for z in range(NZ):
                for c in range(2):
                    yield x, y, z, c


def place(x, y, z, base):
    dz = z ^ base
    far = (dz >> 2) & 1
    near = ((dz >> 1) & 1) ^ far
    member = ((x >> 1) & 1) * 4 + ((y >> 1) & 1) * 2 + (z & 1)
    return member * 4 + near * 2 + far


def colour_groups():
    groups = {}
    for x, y, z, c in coords():
        key = ((x ^ z) & 1, (y ^ z) & 1, z >> 1, c)
        member = ((x >> 1) & 1) * 4 + ((y >> 1) & 1) * 2 + (z & 1)
        groups.setdefault(key, [0] * 8)[member] = linear(x, y, z, c)
    return list(groups.values())


def along_z(flip):
    return [(linear(x, y, z, c), linear(x, y, z ^ flip, c)) for x, y, z, c in coords()]


def from_neighbour(axis):
    pairs = []
    for x, y, z, c in coords():
        q = [x, y, z]
        q[axis] += 1 if c == 0 else -1
        pairs.append((linear(x, y, z, c), linear(q[0] % NX, q[1] % NY, q[2] % NZ, c)))
    return pairs


def other_core():
    return [(linear(x, y, z, c), linear(x, y, z, 1 - c)) for x, y, z, c in coords()]


def merge_layer(layer, mx, my, mz, lists, u_ref, before, w_ref, buf, after):
    px = (mx ^ mz) & 1
    py = (my ^ mz) & 1
    base = (mz, mz, mz, (mz - 1 + 2 * layer) & 7)

    b = (mz & 3) * NX + mx
    y = (b >> 1) & 3
    rows = []
    for j in range(8):
        x = j & 3
        z = (b >> 3) * 4 + (b & 1) * 2 + (j >> 2)
        rel = ((x ^ z ^ px) & 1) + 2 * ((y ^ z ^ py) & 1)
        row = lists[0][place(x, y, z, base[0]), H:ROWS]
        for i in range(1, 4):
            row = jnp.where(rel == i, lists[i][place(x, y, z, base[i]), H:ROWS], row)
        rows.append(row.astype(jnp.float32) * 2.0)
    u = jnp.concatenate(rows, axis=0)
    u = jnp.concatenate([u, u], axis=0)
    r = lax.broadcasted_iota(jnp.int32, u.shape, 0) // 64
    c = lax.broadcasted_iota(jnp.int32, u.shape, 1) // 64
    u_ref[...] = jnp.where(r == c, u, 0.0).astype(jnp.bfloat16)

    for i in range(CHUNKS):
        u = u_ref[...]
        zh, y1 = i >> 1, i & 1
        before(i)
        for y0 in range(2):
            y = y1 * 2 + y0
            for z1 in range(2):
                for kind in range(2):
                    z0 = py ^ (y0 ^ kind)
                    z = zh * 4 + z1 * 2 + z0
                    first = px ^ z0
                    la, lb = lists[2 * kind], lists[2 * kind + 1]
                    parts = []
                    for xh in range(2):
                        even = la[place(2 * xh, y, z, base[2 * kind]), :H]
                        odd = lb[place(2 * xh, y, z, base[2 * kind + 1]), :H]
                        parts.append(jnp.where(first == 0, even, odd))
                        parts.append(jnp.where(first == 0, odd, even))
                    delta = lax.dot_general(
                        u,
                        jnp.concatenate(parts, axis=0),
                        (((1,), (1,)), ((), ())),
                        preferred_element_type=jnp.float32,
                    )
                    at = pl.ds(pl.multiple_of((y0 * 4 + z1 * 2 + z0) * 256, 256), 256)
                    for p in range(2):
                        w = w_ref[i, p, :, at].astype(jnp.float32)
                        buf[i, p, :, at] = (w + delta[p * 64 : p * 64 + 64]).astype(jnp.bfloat16)
        after(i)


def part(ref, layer, i):
    return ref.at[layer, :, :, pl.ds(i * CHUNK, CHUNK)]


def first_kernel(s_ref, a0, a1, a2, a3, w_ref, o_ref, next_ref, held, buf, u_ref, list_sem, load_sem, next_sem, store_sem):
    layer, mx, my, mz = s_ref[0], s_ref[1], s_ref[2], s_ref[3]
    gets = [
        pltpu.make_async_copy(a, held.at[i], list_sem.at[i]) for i, a in enumerate((a0, a1, a2, a3))
    ]
    for get in gets:
        get.start()

    def load(i):
        return pltpu.make_async_copy(part(w_ref, layer, i), buf.at[i], load_sem.at[i])

    def ahead(i):
        return pltpu.make_async_copy(part(w_ref, 1 - layer, i), next_ref.at[i], next_sem.at[i])

    def store(i):
        return pltpu.make_async_copy(buf.at[i], part(o_ref, layer, i), store_sem.at[i])

    for i in range(CHUNKS):
        load(i).start()
    for i in range(CHUNKS):
        ahead(i).start()
    for get in gets:
        get.wait()
    lists = [held.at[i] for i in range(4)]
    merge_layer(
        layer, mx, my, mz, lists, u_ref,
        lambda i: load(i).wait(), buf, buf, lambda i: store(i).start(),
    )
    for i in range(CHUNKS):
        ahead(i).wait()
        store(i).wait()


def second_kernel(s_ref, a0, a1, a2, a3, w_ref, out_ref, o_ref, buf, u_ref, store_sem):
    layer, mx, my, mz = s_ref[0], s_ref[1], s_ref[2], s_ref[3]

    def store(i):
        return pltpu.make_async_copy(buf.at[i], part(o_ref, layer, i), store_sem.at[i])

    merge_layer(
        layer, mx, my, mz, (a0, a1, a2, a3), u_ref,
        lambda i: None, w_ref, buf, lambda i: store(i).start(),
    )
    for i in range(CHUNKS):
        store(i).wait()


SCALARS = pl.BlockSpec(memory_space=pltpu.SMEM)
INSIDE = pl.BlockSpec(memory_space=pltpu.VMEM)
OUTSIDE = pl.BlockSpec(memory_space=pl.ANY)
PARTS = (CHUNKS, 2, 64, CHUNK)
PARAMS = pltpu.CompilerParams(vmem_limit_bytes=VMEM_LIMIT)
COST = pl.CostEstimate(
    flops=2 * 128 * 128 * 8192, bytes_accessed=6 * 1024 * 1024, transcendentals=0
)


def first(scalars, lists, weight):
    return pl.pallas_call(
        first_kernel,
        in_specs=[SCALARS] + [OUTSIDE] * 5,
        out_specs=[OUTSIDE, INSIDE],
        out_shape=[
            jax.ShapeDtypeStruct(weight.shape, weight.dtype),
            jax.ShapeDtypeStruct(PARTS, weight.dtype),
        ],
        scratch_shapes=[
            pltpu.VMEM((4, 32, ROWS, 128), jnp.bfloat16),
            pltpu.VMEM(PARTS, jnp.bfloat16),
            pltpu.VMEM((128, 128), jnp.bfloat16),
            pltpu.SemaphoreType.DMA((4,)),
            pltpu.SemaphoreType.DMA((CHUNKS,)),
            pltpu.SemaphoreType.DMA((CHUNKS,)),
            pltpu.SemaphoreType.DMA((CHUNKS,)),
        ],
        compiler_params=PARAMS,
        cost_estimate=COST,
    )(scalars, *lists, pltpu.with_memory_space_constraint(weight, pltpu.HBM))


def second(scalars, lists, near, out):
    return pl.pallas_call(
        second_kernel,
        in_specs=[SCALARS] + [INSIDE] * 5 + [OUTSIDE],
        out_specs=OUTSIDE,
        out_shape=jax.ShapeDtypeStruct(out.shape, out.dtype),
        scratch_shapes=[
            pltpu.VMEM(PARTS, jnp.bfloat16),
            pltpu.VMEM((128, 128), jnp.bfloat16),
            pltpu.SemaphoreType.DMA((CHUNKS,)),
        ],
        input_output_aliases={6: 0},
        compiler_params=PARAMS,
        cost_estimate=COST,
    )(scalars, *lists, near, out)


def solution(mesh):
    groups = colour_groups()

    def local(down, up, weight):
        core = lax.axis_index("dp")
        train = lax.axis_index("train")
        tp = lax.axis_index("tp")
        x = tp % NX
        y = train % NY
        z = (train // NY) * 4 + tp // NX

        d = lax.dynamic_index_in_dim(down, core, 0, keepdims=False).reshape(128, H).T
        u = lax.dynamic_index_in_dim(up, core, 0, keepdims=False)
        u = u.transpose(1, 0, 2).reshape(UP, 128)
        mine = jnp.concatenate([d, u], axis=0)

        column = mine[None]
        for flip in (6, 2):
            column = jnp.concatenate([column, lax.ppermute(column, AXES, along_z(flip))], axis=0)
        many = jnp.broadcast_to(column[None], (8, 4, ROWS, 128))
        own = lax.all_to_all(many, AXES, 0, 0, axis_index_groups=groups, tiled=True)
        own = own.reshape(32, ROWS, 128)
        lists = [own] + [lax.ppermute(own, AXES, from_neighbour(a)) for a in range(3)]
        swapped = [lax.ppermute(a, AXES, other_core()) for a in lists]

        here = jnp.stack([core, x, y, z]).astype(jnp.int32)
        there = jnp.stack([1 - core, x, y, z]).astype(jnp.int32)
        out, near = first(here, lists, weight)
        return second(there, swapped, near, out)

    spec = P(None, None, "tp", None)
    return jax.shard_map(
        local,
        mesh=mesh,
        in_specs=(
            P(None, None, None, ("train", "tp")),
            P(None, None, ("train", "tp"), None),
            spec,
        ),
        out_specs=spec,
        check_vma=False,
    )
```

```python
import jax
import jax.numpy as jnp
from jax import lax
from jax.experimental import pallas as pl
from jax.experimental.pallas import tpu as pltpu
from jax.sharding import PartitionSpec as P


AXES = ("train", "tp", "dp")
NX, NY, NZ = 4, 4, 8
H = 64
UP = 8
ROWS = H + UP
CHUNK = 2048
CHUNKS = 4
VMEM_LIMIT = 16 * 1024 * 1024


def linear(x, y, z, c):
    return (((z >> 2) * NY + y) * 16 + (z & 3) * NX + x) * 2 + c


def coords():
    for x in range(NX):
        for y in range(NY):
            for z in range(NZ):
                for c in range(2):
                    yield x, y, z, c


def place(x, y, z, base):
    dz = z ^ base
    far = (dz >> 2) & 1
    near = ((dz >> 1) & 1) ^ far
    member = ((x >> 1) & 1) * 4 + ((y >> 1) & 1) * 2 + (z & 1)
    return member * 4 + near * 2 + far


def colour_groups():
    groups = {}
    for x, y, z, c in coords():
        key = ((x ^ z) & 1, (y ^ z) & 1, z >> 1, c)
        member = ((x >> 1) & 1) * 4 + ((y >> 1) & 1) * 2 + (z & 1)
        groups.setdefault(key, [0] * 8)[member] = linear(x, y, z, c)
    return list(groups.values())


def along_z(flip):
    return [(linear(x, y, z, c), linear(x, y, z ^ flip, c)) for x, y, z, c in coords()]


def from_neighbour(axis):
    pairs = []
    for x, y, z, c in coords():
        q = [x, y, z]
        q[axis] += 1 if c == 0 else -1
        pairs.append((linear(x, y, z, c), linear(q[0] % NX, q[1] % NY, q[2] % NZ, c)))
    return pairs


def other_core():
    return [(linear(x, y, z, c), linear(x, y, z, 1 - c)) for x, y, z, c in coords()]


def fetch_kernel(own_ref, w_ref, o_ref, token_ref, sem):
    copies = [
        pltpu.make_async_copy(part(w_ref, layer, i), o_ref.at[layer, i], sem.at[layer * CHUNKS + i])
        for layer in range(2)
        for i in range(CHUNKS)
    ]
    for copy in copies:
        copy.start()
    token_ref[...] = jnp.zeros_like(token_ref)
    for copy in copies:
        copy.wait()


def part(ref, layer, i):
    return ref.at[layer, :, :, pl.ds(i * CHUNK, CHUNK)]


def fetch(own, weight):
    inside = pl.BlockSpec(memory_space=pltpu.VMEM)
    outside = pl.BlockSpec(memory_space=pl.ANY)
    return pl.pallas_call(
        fetch_kernel,
        in_specs=[outside] * 2,
        out_specs=[inside] * 2,
        out_shape=[
            jax.ShapeDtypeStruct((2, CHUNKS, 2, 64, CHUNK), weight.dtype),
            jax.ShapeDtypeStruct((8, 128), jnp.float32),
        ],
        scratch_shapes=[pltpu.SemaphoreType.DMA((2 * CHUNKS,))],
        compiler_params=pltpu.CompilerParams(vmem_limit_bytes=VMEM_LIMIT),
        cost_estimate=pl.CostEstimate(flops=0, bytes_accessed=8 * 1024 * 1024, transcendentals=0),
    )(own, pltpu.with_memory_space_constraint(weight, pltpu.HBM))


def merge_kernel(s_ref, a0, a1, a2, a3, w_ref, *rest):
    lists = (a0, a1, a2, a3)
    o_ref, buf, u_ref, sem = rest[-4:]
    layer, mx, my, mz = s_ref[0], s_ref[1], s_ref[2], s_ref[3]
    px = (mx ^ mz) & 1
    py = (my ^ mz) & 1
    base = (mz, mz, mz, (mz - 1 + 2 * layer) & 7)

    def take(i, x, y, z, rows):
        return lists[i][place(x, y, z, base[i]), rows]

    b = (mz & 3) * NX + mx
    y = (b >> 1) & 3
    rows = []
    for j in range(8):
        x = j & 3
        z = (b >> 3) * 4 + (b & 1) * 2 + (j >> 2)
        rel = ((x ^ z ^ px) & 1) + 2 * ((y ^ z ^ py) & 1)
        row = take(0, x, y, z, slice(H, ROWS))
        for i in range(1, 4):
            row = jnp.where(rel == i, take(i, x, y, z, slice(H, ROWS)), row)
        rows.append(row.astype(jnp.float32) * 2.0)
    u = jnp.concatenate(rows, axis=0)
    u = jnp.concatenate([u, u], axis=0)
    r = lax.broadcasted_iota(jnp.int32, u.shape, 0) // 64
    c = lax.broadcasted_iota(jnp.int32, u.shape, 1) // 64
    u_ref[...] = jnp.where(r == c, u, 0.0).astype(jnp.bfloat16)

    def store(i):
        return pltpu.make_async_copy(buf.at[i], part(o_ref, layer, i), sem.at[i])

    for i in range(CHUNKS):
        u = u_ref[...]
        zh, y1 = i >> 1, i & 1
        for y0 in range(2):
            y = y1 * 2 + y0
            for z1 in range(2):
                for kind in range(2):
                    z0 = py ^ (y0 ^ kind)
                    z = zh * 4 + z1 * 2 + z0
                    first = px ^ z0
                    parts = []
                    for xh in range(2):
                        even = take(2 * kind, 2 * xh, y, z, slice(0, H))
                        odd = take(2 * kind + 1, 2 * xh, y, z, slice(0, H))
                        parts.append(jnp.where(first == 0, even, odd))
                        parts.append(jnp.where(first == 0, odd, even))
                    delta = lax.dot_general(
                        u,
                        jnp.concatenate(parts, axis=0),
                        (((1,), (1,)), ((), ())),
                        preferred_element_type=jnp.float32,
                    )
                    at = pl.ds(pl.multiple_of((y0 * 4 + z1 * 2 + z0) * 256, 256), 256)
                    for p in range(2):
                        w = w_ref[layer, i, p, :, at].astype(jnp.float32)
                        buf[i, p, :, at] = (w + delta[p * 64 : p * 64 + 64]).astype(jnp.bfloat16)
        store(i).start()
    for i in range(CHUNKS):
        store(i).wait()


def merge(scalars, lists, near, shape, out=None):
    inside = pl.BlockSpec(memory_space=pltpu.VMEM)
    outside = pl.BlockSpec(memory_space=pl.ANY)
    args = [scalars, *lists, near]
    in_specs = [pl.BlockSpec(memory_space=pltpu.SMEM)] + [inside] * (len(args) - 1)
    aliases = {}
    if out is not None:
        aliases = {len(args): 0}
        in_specs.append(outside)
        args.append(out)
    return pl.pallas_call(
        merge_kernel,
        in_specs=in_specs,
        out_specs=outside,
        out_shape=jax.ShapeDtypeStruct(shape, jnp.bfloat16),
        scratch_shapes=[
            pltpu.VMEM((CHUNKS, 2, 64, CHUNK), jnp.bfloat16),
            pltpu.VMEM((128, 128), jnp.bfloat16),
            pltpu.SemaphoreType.DMA((CHUNKS,)),
        ],
        input_output_aliases=aliases,
        compiler_params=pltpu.CompilerParams(vmem_limit_bytes=VMEM_LIMIT),
        cost_estimate=pl.CostEstimate(
            flops=2 * 128 * 128 * 8192, bytes_accessed=6 * 1024 * 1024, transcendentals=0
        ),
    )(*args)


def solution(mesh):
    groups = colour_groups()

    def local(down, up, weight):
        core = lax.axis_index("dp")
        train = lax.axis_index("train")
        tp = lax.axis_index("tp")
        x = tp % NX
        y = train % NY
        z = (train // NY) * 4 + tp // NX

        d = lax.dynamic_index_in_dim(down, core, 0, keepdims=False).reshape(128, H).T
        u = lax.dynamic_index_in_dim(up, core, 0, keepdims=False)
        u = u.transpose(1, 0, 2).reshape(UP, 128)
        mine = jnp.concatenate([d, u], axis=0)

        here = jnp.stack([core, x, y, z]).astype(jnp.int32)
        there = jnp.stack([1 - core, x, y, z]).astype(jnp.int32)
        mine, here, there = lax.optimization_barrier((mine, here, there))

        column = mine[None]
        for flip in (6, 2):
            column = jnp.concatenate([column, lax.ppermute(column, AXES, along_z(flip))], axis=0)
        many = jnp.broadcast_to(column[None], (8, 4, ROWS, 128))
        own = lax.all_to_all(many, AXES, 0, 0, axis_index_groups=groups, tiled=True)
        own = own.reshape(32, ROWS, 128)
        near, token = fetch(own, weight)
        lists = [lax.ppermute(own, AXES, from_neighbour(a)) for a in range(3)]
        lists = [own] + [lax.optimization_barrier((token, a))[1] for a in lists]
        swapped = [lax.ppermute(a, AXES, other_core()) for a in lists]

        out = merge(here, lists, near, weight.shape)
        return merge(there, swapped, near, weight.shape, out)

    spec = P(None, None, "tp", None)
    return jax.shard_map(
        local,
        mesh=mesh,
        in_specs=(
            P(None, None, None, ("train", "tp")),
            P(None, None, ("train", "tp"), None),
            spec,
        ),
        out_specs=spec,
        check_vma=False,
    )
```

```python
import jax
import jax.numpy as jnp
from jax import lax
from jax.experimental import pallas as pl
from jax.experimental.pallas import tpu as pltpu
from jax.sharding import PartitionSpec as P


AXES = ("train", "tp", "dp")
NX, NY, NZ = 4, 4, 8
H = 64
UP = 8
ROWS = H + UP
CHUNK = 2048
CHUNKS = 4
VMEM_LIMIT = 16 * 1024 * 1024


def linear(x, y, z, c):
    return (((z >> 2) * NY + y) * 16 + (z & 3) * NX + x) * 2 + c


def coords():
    for x in range(NX):
        for y in range(NY):
            for z in range(NZ):
                for c in range(2):
                    yield x, y, z, c


def place(x, y, z, base):
    dz = z ^ base
    far = (dz >> 2) & 1
    near = ((dz >> 1) & 1) ^ far
    member = ((x >> 1) & 1) * 4 + ((y >> 1) & 1) * 2 + (z & 1)
    return member * 4 + near * 2 + far


def colour_groups():
    groups = {}
    for x, y, z, c in coords():
        key = ((x ^ z) & 1, (y ^ z) & 1, z >> 1, c)
        member = ((x >> 1) & 1) * 4 + ((y >> 1) & 1) * 2 + (z & 1)
        groups.setdefault(key, [0] * 8)[member] = linear(x, y, z, c)
    return list(groups.values())


def along_z(flip):
    return [(linear(x, y, z, c), linear(x, y, z ^ flip, c)) for x, y, z, c in coords()]


def from_neighbour(axis):
    pairs = []
    for x, y, z, c in coords():
        q = [x, y, z]
        q[axis] += 1 if c == 0 else -1
        pairs.append((linear(x, y, z, c), linear(q[0] % NX, q[1] % NY, q[2] % NZ, c)))
    return pairs


def other_core():
    return [(linear(x, y, z, c), linear(x, y, z, 1 - c)) for x, y, z, c in coords()]


def fetch_kernel(own_ref, w_ref, o_ref, token_ref, sem):
    copies = [
        pltpu.make_async_copy(part(w_ref, layer, i), o_ref.at[layer, i], sem.at[layer * CHUNKS + i])
        for layer in range(2)
        for i in range(CHUNKS)
    ]
    for copy in copies:
        copy.start()
    token_ref[...] = jnp.zeros_like(token_ref)
    for copy in copies:
        copy.wait()


def part(ref, layer, i):
    return ref.at[layer, :, :, pl.ds(i * CHUNK, CHUNK)]


def fetch(own, weight):
    inside = pl.BlockSpec(memory_space=pltpu.VMEM)
    outside = pl.BlockSpec(memory_space=pl.ANY)
    return pl.pallas_call(
        fetch_kernel,
        in_specs=[outside] * 2,
        out_specs=[inside] * 2,
        out_shape=[
            jax.ShapeDtypeStruct((2, CHUNKS, 2, 64, CHUNK), weight.dtype),
            jax.ShapeDtypeStruct((8, 128), jnp.float32),
        ],
        scratch_shapes=[pltpu.SemaphoreType.DMA((2 * CHUNKS,))],
        compiler_params=pltpu.CompilerParams(vmem_limit_bytes=VMEM_LIMIT),
        cost_estimate=pl.CostEstimate(flops=0, bytes_accessed=8 * 1024 * 1024, transcendentals=0),
    )(own, pltpu.with_memory_space_constraint(weight, pltpu.HBM))


def merge_kernel(s_ref, a0, a1, a2, a3, w_ref, *rest):
    lists = (a0, a1, a2, a3)
    o_ref, buf, u_ref, sem = rest[-4:]
    layer, mx, my, mz = s_ref[0], s_ref[1], s_ref[2], s_ref[3]
    px = (mx ^ mz) & 1
    py = (my ^ mz) & 1
    base = (mz, mz, mz, (mz - 1 + 2 * layer) & 7)

    def take(i, x, y, z, rows):
        return lists[i][place(x, y, z, base[i]), rows]

    b = (mz & 3) * NX + mx
    y = (b >> 1) & 3
    rows = []
    for j in range(8):
        x = j & 3
        z = (b >> 3) * 4 + (b & 1) * 2 + (j >> 2)
        rel = ((x ^ z ^ px) & 1) + 2 * ((y ^ z ^ py) & 1)
        row = take(0, x, y, z, slice(H, ROWS))
        for i in range(1, 4):
            row = jnp.where(rel == i, take(i, x, y, z, slice(H, ROWS)), row)
        rows.append(row.astype(jnp.float32) * 2.0)
    u = jnp.concatenate(rows, axis=0)
    u = jnp.concatenate([u, u], axis=0)
    r = lax.broadcasted_iota(jnp.int32, u.shape, 0) // 64
    c = lax.broadcasted_iota(jnp.int32, u.shape, 1) // 64
    u_ref[...] = jnp.where(r == c, u, 0.0).astype(jnp.bfloat16)

    def store(i):
        return pltpu.make_async_copy(buf.at[i], part(o_ref, layer, i), sem.at[i])

    for i in range(CHUNKS):
        u = u_ref[...]
        zh, y1 = i >> 1, i & 1
        for y0 in range(2):
            y = y1 * 2 + y0
            for z1 in range(2):
                for kind in range(2):
                    z0 = py ^ (y0 ^ kind)
                    z = zh * 4 + z1 * 2 + z0
                    first = px ^ z0
                    parts = []
                    for xh in range(2):
                        even = take(2 * kind, 2 * xh, y, z, slice(0, H))
                        odd = take(2 * kind + 1, 2 * xh, y, z, slice(0, H))
                        parts.append(jnp.where(first == 0, even, odd))
                        parts.append(jnp.where(first == 0, odd, even))
                    delta = lax.dot_general(
                        u,
                        jnp.concatenate(parts, axis=0),
                        (((1,), (1,)), ((), ())),
                        preferred_element_type=jnp.float32,
                    )
                    at = pl.ds(pl.multiple_of((y0 * 4 + z1 * 2 + z0) * 256, 256), 256)
                    for p in range(2):
                        w = w_ref[layer, i, p, :, at].astype(jnp.float32)
                        buf[i, p, :, at] = (w + delta[p * 64 : p * 64 + 64]).astype(jnp.bfloat16)
        store(i).start()
    for i in range(CHUNKS):
        store(i).wait()


def merge(scalars, lists, near, shape, token, out=None):
    inside = pl.BlockSpec(memory_space=pltpu.VMEM)
    outside = pl.BlockSpec(memory_space=pl.ANY)
    args = [scalars, *lists, near]
    in_specs = [pl.BlockSpec(memory_space=pltpu.SMEM)] + [inside] * (len(args) - 1)
    args.append(token)
    in_specs.append(outside)
    aliases = {}
    if out is not None:
        aliases = {len(args): 0}
        in_specs.append(outside)
        args.append(out)
    return pl.pallas_call(
        merge_kernel,
        in_specs=in_specs,
        out_specs=outside,
        out_shape=jax.ShapeDtypeStruct(shape, jnp.bfloat16),
        scratch_shapes=[
            pltpu.VMEM((CHUNKS, 2, 64, CHUNK), jnp.bfloat16),
            pltpu.VMEM((128, 128), jnp.bfloat16),
            pltpu.SemaphoreType.DMA((CHUNKS,)),
        ],
        input_output_aliases=aliases,
        compiler_params=pltpu.CompilerParams(vmem_limit_bytes=VMEM_LIMIT),
        cost_estimate=pl.CostEstimate(
            flops=2 * 128 * 128 * 8192, bytes_accessed=6 * 1024 * 1024, transcendentals=0
        ),
    )(*args)


def solution(mesh):
    groups = colour_groups()

    def local(down, up, weight):
        core = lax.axis_index("dp")
        train = lax.axis_index("train")
        tp = lax.axis_index("tp")
        x = tp % NX
        y = train % NY
        z = (train // NY) * 4 + tp // NX

        d = lax.dynamic_index_in_dim(down, core, 0, keepdims=False).reshape(128, H).T
        u = lax.dynamic_index_in_dim(up, core, 0, keepdims=False)
        u = u.transpose(1, 0, 2).reshape(UP, 128)
        mine = jnp.concatenate([d, u], axis=0)

        here = jnp.stack([core, x, y, z]).astype(jnp.int32)
        there = jnp.stack([1 - core, x, y, z]).astype(jnp.int32)
        mine, here, there = lax.optimization_barrier((mine, here, there))

        column = mine[None]
        for flip in (6, 2):
            column = jnp.concatenate([column, lax.ppermute(column, AXES, along_z(flip))], axis=0)
        many = jnp.broadcast_to(column[None], (8, 4, ROWS, 128))
        own = lax.all_to_all(many, AXES, 0, 0, axis_index_groups=groups, tiled=True)
        own = own.reshape(32, ROWS, 128)
        near, token = fetch(own, weight)
        lists = [lax.ppermute(own, AXES, from_neighbour(a)) for a in range(3)]
        token, own_after = lax.optimization_barrier((token, own))
        lists = [own] + lists
        swapped = [lax.ppermute(a, AXES, other_core()) for a in (own_after, *lists[1:])]

        out = merge(here, lists, near, weight.shape, token)
        return merge(there, swapped, near, weight.shape, token, out)

    spec = P(None, None, "tp", None)
    return jax.shard_map(
        local,
        mesh=mesh,
        in_specs=(
            P(None, None, None, ("train", "tp")),
            P(None, None, ("train", "tp"), None),
            spec,
        ),
        out_specs=spec,
        check_vma=False,
    )
```

```python
import jax
import jax.numpy as jnp
from jax import lax
from jax.experimental import pallas as pl
from jax.experimental.pallas import tpu as pltpu
from jax.sharding import PartitionSpec as P


AXES = ("train", "tp", "dp")
NX, NY, NZ = 4, 4, 8
H = 64
UP = 8
ROWS = H + UP
CHUNK = 2048
CHUNKS = 4
VMEM_LIMIT = 16 * 1024 * 1024


def linear(x, y, z, c):
    return (((z >> 2) * NY + y) * 16 + (z & 3) * NX + x) * 2 + c


def coords():
    for x in range(NX):
        for y in range(NY):
            for z in range(NZ):
                for c in range(2):
                    yield x, y, z, c


def place(x, y, z, base):
    dz = z ^ base
    far = (dz >> 2) & 1
    near = ((dz >> 1) & 1) ^ far
    member = ((x >> 1) & 1) * 4 + ((y >> 1) & 1) * 2 + (z & 1)
    return member * 4 + near * 2 + far


def colour_groups():
    groups = {}
    for x, y, z, c in coords():
        key = ((x ^ z) & 1, (y ^ z) & 1, z >> 1, c)
        member = ((x >> 1) & 1) * 4 + ((y >> 1) & 1) * 2 + (z & 1)
        groups.setdefault(key, [0] * 8)[member] = linear(x, y, z, c)
    return list(groups.values())


def along_z(flip):
    return [(linear(x, y, z, c), linear(x, y, z ^ flip, c)) for x, y, z, c in coords()]


def from_neighbour(axis):
    pairs = []
    for x, y, z, c in coords():
        q = [x, y, z]
        q[axis] += 1 if c == (axis in (0, 1)) else -1
        pairs.append((linear(x, y, z, c), linear(q[0] % NX, q[1] % NY, q[2] % NZ, c)))
    return pairs


def other_core():
    return [(linear(x, y, z, c), linear(x, y, z, 1 - c)) for x, y, z, c in coords()]


def fetch_kernel(own_ref, w_ref, o_ref, token_ref, sem):
    copies = [
        pltpu.make_async_copy(part(w_ref, layer, i), o_ref.at[layer, i], sem.at[layer * CHUNKS + i])
        for layer in range(2)
        for i in range(CHUNKS)
    ]
    for copy in copies:
        copy.start()
    token_ref[...] = jnp.zeros_like(token_ref)
    for copy in copies:
        copy.wait()


def part(ref, layer, i):
    return ref.at[layer, :, :, pl.ds(i * CHUNK, CHUNK)]


def fetch(own, weight):
    inside = pl.BlockSpec(memory_space=pltpu.VMEM)
    outside = pl.BlockSpec(memory_space=pl.ANY)
    return pl.pallas_call(
        fetch_kernel,
        in_specs=[outside] * 2,
        out_specs=[inside] * 2,
        out_shape=[
            jax.ShapeDtypeStruct((2, CHUNKS, 2, 64, CHUNK), weight.dtype),
            jax.ShapeDtypeStruct((8, 128), jnp.float32),
        ],
        scratch_shapes=[pltpu.SemaphoreType.DMA((2 * CHUNKS,))],
        compiler_params=pltpu.CompilerParams(vmem_limit_bytes=VMEM_LIMIT),
        cost_estimate=pl.CostEstimate(flops=0, bytes_accessed=8 * 1024 * 1024, transcendentals=0),
    )(own, pltpu.with_memory_space_constraint(weight, pltpu.HBM))


def merge_kernel(s_ref, a0, a1, a2, a3, w_ref, *rest):
    lists = (a0, a1, a2, a3)
    o_ref, buf, u_ref, sem = rest[-4:]
    layer, mx, my, mz = s_ref[0], s_ref[1], s_ref[2], s_ref[3]
    px = (mx ^ mz) & 1
    py = (my ^ mz) & 1
    base = (mz, mz, mz, (mz - 1 + 2 * layer) & 7)

    def take(i, x, y, z, rows):
        return lists[i][place(x, y, z, base[i]), rows]

    b = (mz & 3) * NX + mx
    y = (b >> 1) & 3
    rows = []
    for j in range(8):
        x = j & 3
        z = (b >> 3) * 4 + (b & 1) * 2 + (j >> 2)
        rel = ((x ^ z ^ px) & 1) + 2 * ((y ^ z ^ py) & 1)
        row = take(0, x, y, z, slice(H, ROWS))
        for i in range(1, 4):
            row = jnp.where(rel == i, take(i, x, y, z, slice(H, ROWS)), row)
        rows.append(row.astype(jnp.float32) * 2.0)
    u = jnp.concatenate(rows, axis=0)
    u = jnp.concatenate([u, u], axis=0)
    r = lax.broadcasted_iota(jnp.int32, u.shape, 0) // 64
    c = lax.broadcasted_iota(jnp.int32, u.shape, 1) // 64
    u_ref[...] = jnp.where(r == c, u, 0.0).astype(jnp.bfloat16)

    def store(i, y0):
        column = i * CHUNK + y0 * (CHUNK // 2)
        return pltpu.make_async_copy(
            buf.at[i, :, :, pl.ds(y0 * (CHUNK // 2), CHUNK // 2)],
            o_ref.at[layer, :, :, pl.ds(column, CHUNK // 2)],
            sem.at[2 * i + y0],
        )

    for i in range(CHUNKS):
        u = u_ref[...]
        zh, y1 = i >> 1, i & 1
        for y0 in range(2):
            y = y1 * 2 + y0
            for z1 in range(2):
                for kind in range(2):
                    z0 = py ^ (y0 ^ kind)
                    z = zh * 4 + z1 * 2 + z0
                    first = px ^ z0
                    parts = []
                    for xh in range(2):
                        even = take(2 * kind, 2 * xh, y, z, slice(0, H))
                        odd = take(2 * kind + 1, 2 * xh, y, z, slice(0, H))
                        parts.append(jnp.where(first == 0, even, odd))
                        parts.append(jnp.where(first == 0, odd, even))
                    delta = lax.dot_general(
                        u,
                        jnp.concatenate(parts, axis=0),
                        (((1,), (1,)), ((), ())),
                        preferred_element_type=jnp.float32,
                    )
                    at = pl.ds(pl.multiple_of((y0 * 4 + z1 * 2 + z0) * 256, 256), 256)
                    for p in range(2):
                        w = w_ref[layer, i, p, :, at].astype(jnp.float32)
                        buf[i, p, :, at] = (w + delta[p * 64 : p * 64 + 64]).astype(jnp.bfloat16)
            store(i, y0).start()
    for i in range(CHUNKS):
        for y0 in range(2):
            store(i, y0).wait()


def merge(scalars, lists, near, shape, token, out=None):
    inside = pl.BlockSpec(memory_space=pltpu.VMEM)
    outside = pl.BlockSpec(memory_space=pl.ANY)
    args = [scalars, *lists, near]
    in_specs = [pl.BlockSpec(memory_space=pltpu.SMEM)] + [inside] * (len(args) - 1)
    args.append(token)
    in_specs.append(outside)
    aliases = {}
    if out is not None:
        aliases = {len(args): 0}
        in_specs.append(outside)
        args.append(out)
    return pl.pallas_call(
        merge_kernel,
        in_specs=in_specs,
        out_specs=outside,
        out_shape=jax.ShapeDtypeStruct(shape, jnp.bfloat16),
        scratch_shapes=[
            pltpu.VMEM((CHUNKS, 2, 64, CHUNK), jnp.bfloat16),
            pltpu.VMEM((128, 128), jnp.bfloat16),
            pltpu.SemaphoreType.DMA((2 * CHUNKS,)),
        ],
        input_output_aliases=aliases,
        compiler_params=pltpu.CompilerParams(vmem_limit_bytes=VMEM_LIMIT),
        cost_estimate=pl.CostEstimate(
            flops=2 * 128 * 128 * 8192, bytes_accessed=6 * 1024 * 1024, transcendentals=0
        ),
    )(*args)


def solution(mesh):
    groups = colour_groups()

    def local(down, up, weight):
        core = lax.axis_index("dp")
        train = lax.axis_index("train")
        tp = lax.axis_index("tp")
        x = tp % NX
        y = train % NY
        z = (train // NY) * 4 + tp // NX

        d = lax.dynamic_index_in_dim(down, core, 0, keepdims=False).reshape(128, H).T
        u = lax.dynamic_index_in_dim(up, core, 0, keepdims=False)
        u = u.transpose(1, 0, 2).reshape(UP, 128)
        mine = jnp.concatenate([d, u], axis=0)

        here = jnp.stack([core, x, y, z]).astype(jnp.int32)
        there = jnp.stack([1 - core, x, y, z]).astype(jnp.int32)
        mine, here, there = lax.optimization_barrier((mine, here, there))

        column = mine[None]
        for flip in (6, 2):
            column = jnp.concatenate([column, lax.ppermute(column, AXES, along_z(flip))], axis=0)
        many = jnp.broadcast_to(column[None], (8, 4, ROWS, 128))
        own = lax.all_to_all(many, AXES, 0, 0, axis_index_groups=groups, tiled=True)
        own = own.reshape(32, ROWS, 128)
        near, token = fetch(own, weight)
        lists = [lax.ppermute(own, AXES, from_neighbour(a)) for a in range(3)]
        token, own_after = lax.optimization_barrier((token, own))
        lists = [own] + lists
        swapped = [lax.ppermute(a, AXES, other_core()) for a in (own_after, *lists[1:])]

        out = merge(here, lists, near, weight.shape, token)
        return merge(there, swapped, near, weight.shape, token, out)

    spec = P(None, None, "tp", None)
    return jax.shard_map(
        local,
        mesh=mesh,
        in_specs=(
            P(None, None, None, ("train", "tp")),
            P(None, None, ("train", "tp"), None),
            spec,
        ),
        out_specs=spec,
        check_vma=False,
    )
```
